512 devices in a mesh: fsdp: 32 (over z_lo, y), mp: 16 (over x, z_hi, core).
Axes of the slice: x: 4, y: 8, z: 8 (z_hi: 2, z_lo: 4; z = z_hi * 4 + z_lo), core: 2. Of those that a mesh axis runs over, the one named last changes fastest.
Arguments:
- tokens: bfloat16 [6144, 3072], P('fsdp'), may hold values from -6 to 6
- pre_act: bfloat16 [6144, 12288], P('fsdp', 'mp'), may hold values from -6 to 6
- grad_act: bfloat16 [6144, 12288], P('fsdp', 'mp'), may hold values from -6 to 6
- w_up: bfloat16 [3072, 12288], P('fsdp', 'mp'), may hold values from -0.109375 to 0.109375
Outputs:
- grad_weight: bfloat16 [3072, 12288], P('fsdp', 'mp')
- grad_input: bfloat16 [6144, 3072], P('fsdp')
The draws below stay inside these ranges and needn't reach their ends.
All inputs are finite; a program needn't handle non-finite values.
Results may differ from the reference program's by a relative error of at most 0.022.
Values may be sent and summed in bfloat16 or wider, within the bound.
No kernel may reach another device: no remote copies, remote signals or barrier semaphores. Data moves between devices by JAX's collectives and lax.ppermute only.
A program may use at most 64 MiB of HBM per device.

```python
import math
import jax
import jax.numpy as jnp
from jax import lax

D = 3072
FF = 12288
TOKENS = 6144
N_MP = 16


def strengthened(values, key, source, target, parts, factor):
    def block_of(position):
        return (jnp.arange(values.shape[position]) // (values.shape[position] // parts)).reshape((-1,) + (1,) * (values.ndim - 1 - position))

    first = jax.random.permutation(key, parts)[block_of(target)]
    far = (block_of(target) + parts // 2) % parts
    return jnp.where((block_of(source) == first) | (block_of(source) == far), factor * values, values)


def level_of(stream_key, extent, split, smallest, top_value):
    level, own = 1.0, jax.random.fold_in(stream_key, 6)
    for position, shards_of in split:
        steps = jnp.exp(jax.random.uniform(jax.random.fold_in(own, position), (shards_of,), jnp.float32, smallest / len(split), top_value / len(split)))
        level = level * jnp.repeat(steps, extent[position] // shards_of).reshape([-1 if axis == position else 1 for axis in range(len(extent))])
    return level


def normal_values(own_key, extent, deviation, most, shards=(), kind=jnp.bfloat16):
    level = level_of(own_key, extent, shards, -0.22, 0.18) if shards else 1.0
    array = jax.random.normal(own_key, extent, jnp.float32) * deviation * level
    return jnp.minimum(jnp.maximum(array, -most), most).astype(kind)


def noise_with(rng, shape, width, reach, split, heavy, held_as=jnp.bfloat16):
    values = width * jax.random.normal(rng, shape, jnp.float32)
    if split:
        values = values * level_of(rng, shape, split, -0.22, 0.18)
    return jnp.clip(strengthened(values, jax.random.fold_in(rng, 3), *heavy), -reach, reach).astype(held_as)


def setup_inputs(seed: int = 0) -> dict:
    streams_of = jax.random.split(jax.random.key(seed), 5)
    return {
        "tokens": noise_with(streams_of[0], (TOKENS, D), 1.0, 6.0, ((0, 32),), (0, 1, 32, 2.75)),
        "pre_act": normal_values(streams_of[1], (TOKENS, FF), 1.5, 6.0, ((0, 32), (1, 16))),
        "grad_act": normal_values(streams_of[2], (TOKENS, FF), 1.0, 6.0, ((0, 32), (1, 16))),
        "w_up": normal_values(streams_of[3], (D, FF), D ** -0.5, 0.109375, ((0, 32), (1, 16))),
    }


def gelu_slope(hidden):
    coeff = math.sqrt(2.0 / math.pi)
    inner = coeff * (hidden + 0.044715 * hidden * hidden * hidden)
    tangent = jnp.tanh(inner)
    return 0.5 * (1.0 + tangent) + 0.5 * hidden * (1.0 - tangent * tangent) * coeff * (1.0 + 3.0 * 0.044715 * hidden * hidden)

def reference(tokens, pre_act, grad_act, w_up):
    hidden_grad = (grad_act.astype(jnp.float32) * gelu_slope(pre_act.astype(jnp.float32))).astype(jnp.bfloat16)
    weight_sum = jnp.dot(tokens.T, hidden_grad, preferred_element_type=jnp.float32)
    grad_weight = (weight_sum * TOKENS ** (-0.5)).astype(jnp.bfloat16)
    block_width = FF // N_MP
    grad_blocks = hidden_grad.reshape(TOKENS, N_MP, block_width).transpose(1, 0, 2)
    weight_blocks = w_up.reshape(D, N_MP, block_width).transpose(1, 0, 2)

    def add_block(running, pair):
        partial_term = jnp.dot(pair[0], pair[1].T, preferred_element_type=jnp.float32).astype(jnp.bfloat16)
        partial_term = lax.optimization_barrier(partial_term)
        return (running + partial_term.astype(jnp.float32), None)
    zero_sum = jnp.zeros((TOKENS, D), jnp.float32)
    input_sum, unused = lax.scan(add_block, zero_sum, (grad_blocks, weight_blocks))
    return (grad_weight, input_sum.astype(jnp.bfloat16))
```

```python
import math

import jax
import jax.numpy as jnp
from jax import lax
from jax.sharding import PartitionSpec as P

Z_LO, Y = 4, 8
X, Z_HI, CORE = 4, 2, 2


def fsdp_index(z, y):
    return z * Y + y


def mp_index(x, h, c):
    return (x * Z_HI + h) * CORE + c


Y_GROUPS = [[fsdp_index(z, y) for y in range(Y)] for z in range(Z_LO)]
Z_GROUPS = [[fsdp_index(z, y) for z in range(Z_LO)] for y in range(Y)]
X_GROUPS = [[mp_index(x, h, c) for x in range(X)] for h in range(Z_HI) for c in range(CORE)]
C_GROUPS = [[mp_index(x, h, c) for c in range(CORE)] for x in range(X) for h in range(Z_HI)]
RING_GROUPS = [
    [fsdp_index(z, y) * (X * Z_HI * CORE) + mp_index(x, h, c) for h in range(Z_HI) for z in range(Z_LO)]
    for y in range(Y)
    for x in range(X)
    for c in range(CORE)
]


def gelu_slope(hidden):
    coeff = math.sqrt(2.0 / math.pi)
    inner = coeff * (hidden + 0.044715 * hidden * hidden * hidden)
    tangent = jnp.tanh(inner)
    return 0.5 * (1.0 + tangent) + 0.5 * hidden * (1.0 - tangent * tangent) * coeff * (
        1.0 + 3.0 * 0.044715 * hidden * hidden
    )


def swap(blocks, axis, groups):
    return lax.all_to_all(blocks, axis, 0, 0, axis_index_groups=groups, tiled=True)


def added(blocks):
    return jnp.sum(blocks.astype(jnp.float32), axis=0).astype(jnp.bfloat16)


def shards(tokens, pre_act, grad_act, w_up):
    rows, width = tokens.shape
    units = pre_act.shape[1]
    quarter = width // Z_LO
    norm_factor = float(rows * Z_LO * Y) ** (-0.5)

    weight = lax.all_gather(w_up, "fsdp", axis=0, axis_index_groups=Y_GROUPS, tiled=True)
    hidden_grad = (grad_act.astype(jnp.float32) * gelu_slope(pre_act.astype(jnp.float32))).astype(
        jnp.bfloat16
    )
    hidden = swap(jnp.broadcast_to(hidden_grad[None], (Z_LO, rows, units)), "fsdp", Z_GROUPS)
    hidden = hidden.reshape(Z_LO * rows, units)
    patches = swap(tokens.reshape(rows, Z_LO, quarter).transpose(1, 0, 2), "fsdp", Z_GROUPS)
    patches = patches.reshape(Z_LO * rows, quarter)

    weight_part = lax.dot_general(
        patches, hidden, (((0,), (0,)), ((), ())), preferred_element_type=jnp.float32
    ).astype(jnp.bfloat16)
    received = swap(weight_part.reshape(Y, quarter // Y, units), "fsdp", Y_GROUPS)
    grad_weight = (jnp.sum(received.astype(jnp.float32), axis=0) * norm_factor).astype(jnp.bfloat16)

    partial = lax.dot_general(
        hidden, weight, (((1,), (1,)), ((), ())), preferred_element_type=jnp.float32
    ).astype(jnp.bfloat16)
    piece = rows // (CORE * X)
    partial = partial.reshape(Z_LO, CORE, X, piece, quarter).transpose(1, 2, 0, 3, 4)
    partial = added(swap(partial, "mp", C_GROUPS).reshape(CORE, X, Z_LO, piece, quarter))
    partial = added(swap(partial, "mp", X_GROUPS))
    both = jnp.broadcast_to(partial[None], (Z_HI, Z_LO, piece, quarter))
    both = swap(both.reshape(Z_HI * Z_LO, piece, quarter), ("fsdp", "mp"), RING_GROUPS)
    mine = added(both.reshape(Z_HI, Z_LO, piece, quarter))
    mine = mine.transpose(1, 0, 2).reshape(piece, width)
    mine = lax.all_gather(mine, "mp", axis=0, axis_index_groups=X_GROUPS, tiled=True)
    half = jnp.broadcast_to(mine[None], (CORE, X * piece, width))
    grad_input = swap(half, "mp", C_GROUPS).reshape(rows, width)
    return (grad_weight, grad_input)


def solution(mesh):
    placed = (P("fsdp", None), P("fsdp", "mp"), P("fsdp", "mp"), P("fsdp", "mp"))
    return jax.shard_map(
        shards,
        mesh=mesh,
        in_specs=placed,
        out_specs=(P("fsdp", "mp"), P("fsdp", None)),
        check_vma=False,
    )
```

```python
import math

import jax
import jax.numpy as jnp
from jax import lax
from jax.sharding import PartitionSpec as P

Z_LO, Y = 4, 8
X, Z_HI, CORE = 4, 2, 2
AXES = ("fsdp", "mp")


def fsdp_index(z, y):
    return z * Y + y


def mp_index(x, h, c):
    return (x * Z_HI + h) * CORE + c


Y_GROUPS = [[fsdp_index(z, y) for y in range(Y)] for z in range(Z_LO)]


def moved(value, target):
    pairs = []
    for z in range(Z_LO):
        for y in range(Y):
            for x in range(X):
                for h in range(Z_HI):
                    for c in range(CORE):
                        z2, y2, x2, h2, c2 = target(z, y, x, h, c)
                        source = fsdp_index(z, y) * X * Z_HI * CORE + mp_index(x, h, c)
                        goal = fsdp_index(z2, y2) * X * Z_HI * CORE + mp_index(x2, h2, c2)
                        pairs.append((source, goal))
    return lax.ppermute(value, AXES, pairs)


def along_z_lo(value, step):
    return moved(value, lambda z, y, x, h, c: ((z + step) % Z_LO, y, x, h, c))


def along_ring(value, step):
    def target(z, y, x, h, c):
        place = (h * Z_LO + z + step) % (Z_HI * Z_LO)
        return place % Z_LO, y, x, place // Z_LO, c

    return moved(value, target)


def along_x(value, step):
    return moved(value, lambda z, y, x, h, c: (z, y, (x + step) % X, h, c))


def to_other_core(value):
    return moved(value, lambda z, y, x, h, c: (z, y, x, h, 1 - c))


def gelu_slope(hidden):
    coeff = math.sqrt(2.0 / math.pi)
    inner = coeff * (hidden + 0.044715 * hidden * hidden * hidden)
    tangent = jnp.tanh(inner)
    return 0.5 * (1.0 + tangent) + 0.5 * hidden * (1.0 - tangent * tangent) * coeff * (
        1.0 + 3.0 * 0.044715 * hidden * hidden
    )


def swap(blocks, axis, groups):
    return lax.all_to_all(blocks, axis, 0, 0, axis_index_groups=groups, tiled=True)


def total(parts):
    result = parts[0].astype(jnp.float32)
    for part in parts[1:]:
        result = result + part.astype(jnp.float32)
    return result.astype(jnp.bfloat16)


def canonical(blocks, shift, axis):
    n = blocks.shape[axis]
    doubled = jnp.concatenate([jnp.flip(blocks, axis)] * 2, axis)
    return lax.dynamic_slice_in_dim(doubled, (n - 1 - shift) % n, n, axis)


def shards(tokens, pre_act, grad_act, w_up):
    rows, width = tokens.shape
    units = pre_act.shape[1]
    quarter = width // Z_LO
    half = quarter // CORE
    norm_factor = float(rows * Z_LO * Y) ** (-0.5)
    z_lo = lax.axis_index("fsdp") // Y
    x = lax.axis_index("mp") // (Z_HI * CORE)
    core = lax.axis_index("mp") % CORE

    weight = swap(jnp.broadcast_to(w_up[None], (Y,) + w_up.shape), "fsdp", Y_GROUPS)
    weight = weight.reshape(quarter, units)
    hidden_grad = (grad_act.astype(jnp.float32) * gelu_slope(pre_act.astype(jnp.float32))).astype(
        jnp.bfloat16
    )
    hidden = jnp.stack([hidden_grad] + [along_z_lo(hidden_grad, k) for k in range(1, Z_LO)])
    mine = lax.dynamic_slice_in_dim(tokens, core * (rows // CORE), rows // CORE, 0)
    mine = [
        lax.dynamic_slice_in_dim(mine, ((z_lo + k) % Z_LO) * quarter, quarter, 1) for k in range(Z_LO)
    ]
    mine = jnp.stack([mine[0]] + [along_z_lo(mine[k], k) for k in range(1, Z_LO)])
    other = to_other_core(mine)
    patches = jnp.where(
        core == 0, jnp.stack([mine, other], axis=1), jnp.stack([other, mine], axis=1)
    ).reshape(Z_LO * rows, quarter)
    hidden = hidden.reshape(Z_LO * rows, units)

    weight_part = lax.dot_general(
        patches, hidden, (((0,), (0,)), ((), ())), preferred_element_type=jnp.float32
    ).astype(jnp.bfloat16)
    received = swap(weight_part.reshape(Y, quarter // Y, units), "fsdp", Y_GROUPS)
    grad_weight = (jnp.sum(received.astype(jnp.float32), axis=0) * norm_factor).astype(jnp.bfloat16)

    def partial_of(which):
        chosen = lax.dynamic_slice_in_dim(weight, which * half, half, 0)
        return lax.dot_general(
            hidden, chosen, (((1,), (1,)), ((), ())), preferred_element_type=jnp.float32
        ).astype(jnp.bfloat16)

    theirs = to_other_core(partial_of(1 - core))
    partial = total([partial_of(core), theirs])
    piece = rows // X
    partial = partial.reshape(Z_LO, X, piece, half)
    pieces = [
        lax.dynamic_slice_in_dim(partial, (x + j) % X, 1, 1).reshape(Z_LO, piece, half) for j in range(X)
    ]
    partial = total([pieces[0]] + [along_x(pieces[j], j) for j in range(1, X)])
    ring = [partial[0]] + [along_ring(partial[-m % Z_LO], m) for m in range(1, Z_HI * Z_LO)]
    ring = jnp.stack([total([ring[m], ring[m + Z_LO]]) for m in range(Z_LO)])
    ring = canonical(ring, z_lo, 0).transpose(1, 0, 2).reshape(piece, Z_LO * half)
    gathered = jnp.stack([ring] + [along_x(ring, j) for j in range(1, X)])
    theirs = to_other_core(gathered)
    gathered = canonical(gathered, x, 0).reshape(rows, Z_LO, half)
    theirs = canonical(theirs, x, 0).reshape(rows, Z_LO, half)
    grad_input = jnp.where(
        core == 0, jnp.stack([gathered, theirs], axis=2), jnp.stack([theirs, gathered], axis=2)
    ).reshape(rows, width)
    return (grad_weight, grad_input)


def solution(mesh):
    placed = (P("fsdp", None), P("fsdp", "mp"), P("fsdp", "mp"), P("fsdp", "mp"))
    return jax.shard_map(
        shards,
        mesh=mesh,
        in_specs=placed,
        out_specs=(P("fsdp", "mp"), P("fsdp", None)),
        check_vma=False,
    )
```

```python
import math

import jax
import jax.numpy as jnp
from jax import lax
from jax.sharding import PartitionSpec as P

Z_LO, Y = 4, 8
X, Z_HI, CORE = 4, 2, 2
AXES = ("fsdp", "mp")


def fsdp_index(z, y):
    return z * Y + y


def mp_index(x, h, c):
    return (x * Z_HI + h) * CORE + c


Y_GROUPS = [[fsdp_index(z, y) for y in range(Y)] for z in range(Z_LO)]
X_GROUPS = [[mp_index(x, h, c) for x in range(X)] for h in range(Z_HI) for c in range(CORE)]
RING_GROUPS = [
    [fsdp_index(z, y) * (X * Z_HI * CORE) + mp_index(x, h, c) for h in range(Z_HI) for z in range(Z_LO)]
    for y in range(Y)
    for x in range(X)
    for c in range(CORE)
]


def moved(value, target):
    pairs = []
    for z in range(Z_LO):
        for y in range(Y):
            for x in range(X):
                for h in range(Z_HI):
                    for c in range(CORE):
                        z2, y2, x2, h2, c2 = target(z, y, x, h, c)
                        source = fsdp_index(z, y) * X * Z_HI * CORE + mp_index(x, h, c)
                        goal = fsdp_index(z2, y2) * X * Z_HI * CORE + mp_index(x2, h2, c2)
                        pairs.append((source, goal))
    return lax.ppermute(value, AXES, pairs)


def along_z_lo(value, step):
    return moved(value, lambda z, y, x, h, c: ((z + step) % Z_LO, y, x, h, c))


def along_ring(value, step):
    def target(z, y, x, h, c):
        place = (h * Z_LO + z + step) % (Z_HI * Z_LO)
        return place % Z_LO, y, x, place // Z_LO, c

    return moved(value, target)


def along_x(value, step):
    return moved(value, lambda z, y, x, h, c: (z, y, (x + step) % X, h, c))


def to_other_core(value):
    return moved(value, lambda z, y, x, h, c: (z, y, x, h, 1 - c))


def gelu_slope(hidden):
    coeff = math.sqrt(2.0 / math.pi)
    inner = coeff * (hidden + 0.044715 * hidden * hidden * hidden)
    tangent = jnp.tanh(inner)
    return 0.5 * (1.0 + tangent) + 0.5 * hidden * (1.0 - tangent * tangent) * coeff * (
        1.0 + 3.0 * 0.044715 * hidden * hidden
    )


def swap(blocks, axis, groups):
    return lax.all_to_all(blocks, axis, 0, 0, axis_index_groups=groups, tiled=True)


def total(parts):
    result = parts[0].astype(jnp.float32)
    for part in parts[1:]:
        result = result + part.astype(jnp.float32)
    return result.astype(jnp.bfloat16)


def canonical(blocks, shift, axis):
    n = blocks.shape[axis]
    doubled = jnp.concatenate([jnp.flip(blocks, axis)] * 2, axis)
    return lax.dynamic_slice_in_dim(doubled, (n - 1 - shift) % n, n, axis)


def shards(tokens, pre_act, grad_act, w_up):
    rows, width = tokens.shape
    units = pre_act.shape[1]
    quarter = width // Z_LO
    norm_factor = float(rows * Z_LO * Y) ** (-0.5)
    z_lo = lax.axis_index("fsdp") // Y
    x = lax.axis_index("mp") // (Z_HI * CORE)
    core = lax.axis_index("mp") % CORE

    weight = lax.all_gather(w_up, "fsdp", axis=0, axis_index_groups=Y_GROUPS, tiled=True)
    hidden_grad = (grad_act.astype(jnp.float32) * gelu_slope(pre_act.astype(jnp.float32))).astype(
        jnp.bfloat16
    )
    hidden = [hidden_grad] + [along_z_lo(hidden_grad, k) for k in range(1, Z_LO)]
    hidden = jnp.stack(hidden).reshape(Z_LO * rows, units)
    part = rows // (CORE * X)
    mine = lax.dynamic_slice_in_dim(tokens, (core * X + x) * part, part, 0)
    mine = [
        lax.dynamic_slice_in_dim(mine, ((z_lo + k) % Z_LO) * quarter, quarter, 1) for k in range(Z_LO)
    ]
    mine = jnp.stack([mine[0]] + [along_z_lo(mine[k], k) for k in range(1, Z_LO)])
    mine = lax.all_gather(mine, "mp", axis=1, axis_index_groups=X_GROUPS, tiled=True)
    other = to_other_core(mine)
    patches = jnp.where(
        core == 0, jnp.stack([mine, other], axis=1), jnp.stack([other, mine], axis=1)
    ).reshape(Z_LO * rows, quarter)

    weight_part = lax.dot_general(
        patches, hidden, (((0,), (0,)), ((), ())), preferred_element_type=jnp.float32
    ).astype(jnp.bfloat16)
    received = lax.psum_scatter(
        weight_part, "fsdp", scatter_dimension=0, axis_index_groups=Y_GROUPS, tiled=True
    )
    grad_weight = (received.astype(jnp.float32) * norm_factor).astype(jnp.bfloat16)

    share = rows // CORE
    piece = share // X
    by_core = hidden.reshape(Z_LO, CORE, X, piece, units)

    def partial_of(which):
        chosen = lax.dynamic_slice_in_dim(by_core, which, 1, 1).transpose(1, 2, 0, 3, 4)
        return lax.dot_general(
            chosen.reshape(Z_LO * share, units),
            weight,
            (((1,), (1,)), ((), ())),
            preferred_element_type=jnp.float32,
        )

    theirs = to_other_core(partial_of(1 - core).astype(jnp.bfloat16))
    partial = (partial_of(core) + theirs.astype(jnp.float32)).astype(jnp.bfloat16)
    partial = swap(partial.reshape(X, Z_LO, piece, quarter), "mp", X_GROUPS)
    partial = total([partial[j] for j in range(X)])
    partial = canonical(partial, z_lo, 0)
    both = jnp.concatenate([partial, partial], 0)
    both = swap(both, AXES, RING_GROUPS).reshape(Z_HI, Z_LO, piece, quarter)
    ring = total([both[0], both[1]])
    ring = ring.transpose(1, 0, 2).reshape(piece, width)
    mine = lax.all_gather(ring, "mp", axis=0, axis_index_groups=X_GROUPS, tiled=True)
    theirs = to_other_core(mine)
    grad_input = jnp.where(
        core == 0, jnp.concatenate([mine, theirs], 0), jnp.concatenate([theirs, mine], 0)
    )
    return (grad_weight, grad_input)


def solution(mesh):
    placed = (P("fsdp", None), P("fsdp", "mp"), P("fsdp", "mp"), P("fsdp", "mp"))
    return jax.shard_map(
        shards,
        mesh=mesh,
        in_specs=placed,
        out_specs=(P("fsdp", "mp"), P("fsdp", None)),
        check_vma=False,
    )
```

```python
import math

import jax
import jax.numpy as jnp
from jax import lax
from jax.experimental import pallas as pl
from jax.experimental.pallas import tpu as pltpu
from jax.sharding import PartitionSpec as P

Z_LO, Y = 4, 8
X, Z_HI, CORE = 4, 2, 2
AXES = ("fsdp", "mp")


def fsdp_index(z, y):
    return z * Y + y


def mp_index(x, h, c):
    return (x * Z_HI + h) * CORE + c


Y_GROUPS = [[fsdp_index(z, y) for y in range(Y)] for z in range(Z_LO)]
X_GROUPS = [[mp_index(x, h, c) for x in range(X)] for h in range(Z_HI) for c in range(CORE)]
RING_GROUPS = [
    [fsdp_index(z, y) * (X * Z_HI * CORE) + mp_index(x, h, c) for h in range(Z_HI) for z in range(Z_LO)]
    for y in range(Y)
    for x in range(X)
    for c in range(CORE)
]


def moved(value, target):
    pairs = []
    for z in range(Z_LO):
        for y in range(Y):
            for x in range(X):
                for h in range(Z_HI):
                    for c in range(CORE):
                        z2, y2, x2, h2, c2 = target(z, y, x, h, c)
                        source = fsdp_index(z, y) * X * Z_HI * CORE + mp_index(x, h, c)
                        goal = fsdp_index(z2, y2) * X * Z_HI * CORE + mp_index(x2, h2, c2)
                        pairs.append((source, goal))
    return lax.ppermute(value, AXES, pairs)


def along_z_lo(value, step):
    return moved(value, lambda z, y, x, h, c: ((z + step) % Z_LO, y, x, h, c))


def to_other_core(value):
    return moved(value, lambda z, y, x, h, c: (z, y, x, h, 1 - c))


def gelu_slope(hidden):
    coeff = math.sqrt(2.0 / math.pi)
    inner = coeff * (hidden + 0.044715 * hidden * hidden * hidden)
    tangent = jnp.tanh(inner)
    return 0.5 * (1.0 + tangent) + 0.5 * hidden * (1.0 - tangent * tangent) * coeff * (
        1.0 + 3.0 * 0.044715 * hidden * hidden
    )


def swap(blocks, axis, groups):
    return lax.all_to_all(blocks, axis, 0, 0, axis_index_groups=groups, tiled=True)


def input_parts_kernel(place, *refs):
    blocks, weight, outs = refs[:Z_LO], refs[Z_LO], refs[Z_LO + 1 :]
    rows = blocks[0].shape[0]
    piece = rows // X
    half = weight.shape[0] // CORE
    lhs = jnp.concatenate([block[...] for block in blocks], axis=0)
    for out, which in zip(outs, (1 - place[1], place[1])):
        result = lax.dot_general(
            lhs,
            weight[pl.ds(pl.multiple_of(which * half, half), half), :],
            (((1,), (1,)), ((), ())),
            preferred_element_type=jnp.float32,
        )
        for k in range(Z_LO):
            owner = jnp.bitwise_and(place[0] + (Z_LO - k), Z_LO - 1)
            for x in range(X):
                start = k * rows + x * piece
                out[x, owner] = result[start : start + piece].astype(out.dtype)


def input_parts(place, blocks, weight):
    rows, units = blocks[0].shape
    half = weight.shape[0] // CORE
    out = jax.ShapeDtypeStruct((X, Z_LO, rows // X, half), jnp.bfloat16)
    return pl.pallas_call(
        input_parts_kernel,
        in_specs=[pl.BlockSpec(memory_space=pltpu.SMEM)]
        + [pl.BlockSpec(memory_space=pltpu.VMEM)] * (Z_LO + 1),
        out_specs=[pl.BlockSpec(memory_space=pltpu.VMEM)] * 2,
        out_shape=[out, out],
        compiler_params=pltpu.CompilerParams(vmem_limit_bytes=32 * 1024 * 1024),
        cost_estimate=pl.CostEstimate(
            flops=4 * Z_LO * rows * units * half,
            bytes_accessed=2 * (Z_LO * rows * units + 2 * half * units + 2 * Z_LO * rows * half),
            transcendentals=0,
        ),
    )(place, *blocks, weight)


def joined_kernel(core, mine, theirs, out):
    blocks, quarters, piece, half = mine.shape
    for own in range(CORE):

        @pl.when(core[0] == own)
        def _():
            for x in range(blocks):
                for z in range(quarters):
                    for c in range(CORE):
                        start = (z * CORE + c) * half
                        out[x * piece : (x + 1) * piece, start : start + half] = (
                            mine if c == own else theirs
                        )[x, z]


def joined(core, mine, theirs):
    x, z, piece, half = mine.shape
    return pl.pallas_call(
        joined_kernel,
        in_specs=[
            pl.BlockSpec(memory_space=pltpu.SMEM),
            pl.BlockSpec(memory_space=pltpu.VMEM),
            pl.BlockSpec(memory_space=pltpu.VMEM),
        ],
        out_specs=pl.BlockSpec(memory_space=pltpu.VMEM),
        out_shape=jax.ShapeDtypeStruct((x * piece, z * CORE * half), mine.dtype),
        compiler_params=pltpu.CompilerParams(vmem_limit_bytes=32 * 1024 * 1024),
        cost_estimate=pl.CostEstimate(
            flops=0, bytes_accessed=4 * CORE * mine.size, transcendentals=0
        ),
    )(core, mine, theirs)


def total(blocks):
    return jnp.sum(blocks.astype(jnp.float32), axis=0).astype(jnp.bfloat16)


def shards(tokens, pre_act, grad_act, w_up):
    rows, width = tokens.shape
    units = pre_act.shape[1]
    quarter = width // Z_LO
    half = quarter // CORE
    piece = rows // X
    norm_factor = float(rows * Z_LO * Y) ** (-0.5)
    z_lo = lax.shift_right_logical(lax.axis_index("fsdp"), 3)
    x = lax.shift_right_logical(lax.axis_index("mp"), 2)
    core = jnp.bitwise_and(lax.axis_index("mp"), 1)
    own_place = jnp.stack([z_lo, core])

    weight = lax.all_gather(w_up, "fsdp", axis=0, axis_index_groups=Y_GROUPS, tiled=True)
    hidden_grad = (grad_act.astype(jnp.float32) * gelu_slope(pre_act.astype(jnp.float32))).astype(
        jnp.bfloat16
    )
    hidden = [hidden_grad] + [along_z_lo(hidden_grad, k) for k in range(1, Z_LO)]
    part = rows // (CORE * X)
    mine = lax.dynamic_slice_in_dim(tokens, (core * X + x) * part, part, 0)
    mine = [
        lax.dynamic_slice_in_dim(mine, jnp.bitwise_and(z_lo + k, Z_LO - 1) * quarter, quarter, 1)
        for k in range(Z_LO)
    ]
    mine = jnp.stack([mine[0]] + [along_z_lo(mine[k], k) for k in range(1, Z_LO)])
    mine = lax.all_gather(mine, "mp", axis=1, axis_index_groups=X_GROUPS, tiled=True)
    mine, hidden = lax.optimization_barrier((mine, hidden))
    other = to_other_core(mine)
    patches = jnp.where(
        core == 0, jnp.stack([mine, other], axis=1), jnp.stack([other, mine], axis=1)
    ).reshape(Z_LO * rows, quarter)

    weight_part = lax.dot_general(
        patches,
        jnp.concatenate(hidden, 0),
        (((0,), (0,)), ((), ())),
        preferred_element_type=jnp.float32,
    ).astype(jnp.bfloat16)
    received = lax.psum_scatter(
        weight_part, "fsdp", scatter_dimension=0, axis_index_groups=Y_GROUPS, tiled=True
    )
    grad_weight = (received.astype(jnp.float32) * norm_factor).astype(jnp.bfloat16)

    for_other, for_own = input_parts(own_place, hidden, weight)
    theirs = to_other_core(for_other)
    partial = (for_own.astype(jnp.float32) + theirs.astype(jnp.float32)).astype(jnp.bfloat16)
    partial = total(swap(partial, "mp", X_GROUPS))
    both = jnp.broadcast_to(partial[None], (Z_HI, Z_LO, piece, half))
    both = swap(both.reshape(Z_HI * Z_LO, piece, half), AXES, RING_GROUPS)
    mine = total(both.reshape(Z_HI, Z_LO, piece, half))
    mine = swap(jnp.broadcast_to(mine[None], (X, Z_LO, piece, half)), "mp", X_GROUPS)
    grad_input = joined(core.reshape(1), mine, to_other_core(mine))
    return (grad_weight, grad_input)


def solution(mesh):
    placed = (P("fsdp", None), P("fsdp", "mp"), P("fsdp", "mp"), P("fsdp", "mp"))
    return jax.shard_map(
        shards,
        mesh=mesh,
        in_specs=placed,
        out_specs=(P("fsdp", "mp"), P("fsdp", None)),
        check_vma=False,
    )
```

```python
import math

import jax
import jax.numpy as jnp
from jax import lax
from jax.experimental import pallas as pl
from jax.experimental.pallas import tpu as pltpu
from jax.sharding import PartitionSpec as P

Z_LO, Y = 4, 8
X, Z_HI, CORE = 4, 2, 2
AXES = ("fsdp", "mp")


def fsdp_index(z, y):
    return z * Y + y


def mp_index(x, h, c):
    return (x * Z_HI + h) * CORE + c


Y_GROUPS = [[fsdp_index(z, y) for y in range(Y)] for z in range(Z_LO)]
C_GROUPS = [[mp_index(x, h, c) for c in range(CORE)] for x in range(X) for h in range(Z_HI)]
X_GROUPS = [[mp_index(x, h, c) for x in range(X)] for h in range(Z_HI) for c in range(CORE)]
RING_GROUPS = [
    [fsdp_index(z, y) * (X * Z_HI * CORE) + mp_index(x, h, c) for h in range(Z_HI) for z in range(Z_LO)]
    for y in range(Y)
    for x in range(X)
    for c in range(CORE)
]


def moved(value, target):
    pairs = []
    for z in range(Z_LO):
        for y in range(Y):
            for x in range(X):
                for h in range(Z_HI):
                    for c in range(CORE):
                        z2, y2, x2, h2, c2 = target(z, y, x, h, c)
                        source = fsdp_index(z, y) * X * Z_HI * CORE + mp_index(x, h, c)
                        goal = fsdp_index(z2, y2) * X * Z_HI * CORE + mp_index(x2, h2, c2)
                        pairs.append((source, goal))
    return lax.ppermute(value, AXES, pairs)


def along_z_lo(value, step):
    return moved(value, lambda z, y, x, h, c: ((z + step) % Z_LO, y, x, h, c))


def to_other_core(value):
    return moved(value, lambda z, y, x, h, c: (z, y, x, h, 1 - c))


def gelu_slope(hidden):
    coeff = math.sqrt(2.0 / math.pi)
    inner = coeff * (hidden + 0.044715 * hidden * hidden * hidden)
    tangent = jnp.tanh(inner)
    return 0.5 * (1.0 + tangent) + 0.5 * hidden * (1.0 - tangent * tangent) * coeff * (
        1.0 + 3.0 * 0.044715 * hidden * hidden
    )


def swap(blocks, axis, groups):
    return lax.all_to_all(blocks, axis, 0, 0, axis_index_groups=groups, tiled=True)


def input_parts_kernel(place, *refs):
    blocks, weight, outs = refs[:Z_LO], refs[Z_LO], refs[Z_LO + 1 :]
    rows = blocks[0].shape[0]
    piece = rows // X
    half = weight.shape[0] // CORE
    lhs = jnp.concatenate([block[...] for block in blocks], axis=0)
    for out, which in zip(outs, (1 - place[1], place[1])):
        result = lax.dot_general(
            lhs,
            weight[pl.ds(pl.multiple_of(which * half, half), half), :],
            (((1,), (1,)), ((), ())),
            preferred_element_type=jnp.float32,
        )
        for k in range(Z_LO):
            owner = jnp.bitwise_and(place[0] + (Z_LO - k), Z_LO - 1)
            for x in range(X):
                start = k * rows + x * piece
                out[x, owner] = result[start : start + piece].astype(out.dtype)


def input_parts(place, blocks, weight):
    rows, units = blocks[0].shape
    half = weight.shape[0] // CORE
    out = jax.ShapeDtypeStruct((X, Z_LO, rows // X, half), jnp.bfloat16)
    return pl.pallas_call(
        input_parts_kernel,
        in_specs=[pl.BlockSpec(memory_space=pltpu.SMEM)]
        + [pl.BlockSpec(memory_space=pltpu.VMEM)] * (Z_LO + 1),
        out_specs=[pl.BlockSpec(memory_space=pltpu.VMEM)] * 2,
        out_shape=[out, out],
        compiler_params=pltpu.CompilerParams(vmem_limit_bytes=32 * 1024 * 1024),
        cost_estimate=pl.CostEstimate(
            flops=4 * Z_LO * rows * units * half,
            bytes_accessed=2 * (Z_LO * rows * units + 2 * half * units + 2 * Z_LO * rows * half),
            transcendentals=0,
        ),
    )(place, *blocks, weight)


def joined_kernel(core, mine, theirs, out):
    blocks, quarters, piece, half = mine.shape
    for own in range(CORE):

        @pl.when(core[0] == own)
        def _():
            for x in range(blocks):
                for z in range(quarters):
                    for c in range(CORE):
                        start = (z * CORE + c) * half
                        out[x * piece : (x + 1) * piece, start : start + half] = (
                            mine if c == own else theirs
                        )[x, z]


def joined(core, mine, theirs):
    x, z, piece, half = mine.shape
    return pl.pallas_call(
        joined_kernel,
        in_specs=[
            pl.BlockSpec(memory_space=pltpu.SMEM),
            pl.BlockSpec(memory_space=pltpu.VMEM),
            pl.BlockSpec(memory_space=pltpu.VMEM),
        ],
        out_specs=pl.BlockSpec(memory_space=pltpu.VMEM),
        out_shape=jax.ShapeDtypeStruct((x * piece, z * CORE * half), mine.dtype),
        compiler_params=pltpu.CompilerParams(vmem_limit_bytes=32 * 1024 * 1024),
        cost_estimate=pl.CostEstimate(
            flops=0, bytes_accessed=4 * CORE * mine.size, transcendentals=0
        ),
    )(core, mine, theirs)


def total(blocks):
    return jnp.sum(blocks.astype(jnp.float32), axis=0).astype(jnp.bfloat16)


def shards(tokens, pre_act, grad_act, w_up):
    rows, width = tokens.shape
    units = pre_act.shape[1]
    quarter = width // Z_LO
    half = quarter // CORE
    piece = rows // X
    norm_factor = float(rows * Z_LO * Y) ** (-0.5)
    z_lo = lax.shift_right_logical(lax.axis_index("fsdp"), 3)
    x = lax.shift_right_logical(lax.axis_index("mp"), 2)
    core = jnp.bitwise_and(lax.axis_index("mp"), 1)
    own_place = jnp.stack([z_lo, core])

    weight = lax.all_gather(w_up, "fsdp", axis=0, axis_index_groups=Y_GROUPS, tiled=True)
    hidden_grad = (grad_act.astype(jnp.float32) * gelu_slope(pre_act.astype(jnp.float32))).astype(
        jnp.bfloat16
    )
    part = rows // (CORE * X)
    mine = lax.dynamic_slice_in_dim(tokens, (core * X + x) * part, part, 0)
    mine = [
        lax.dynamic_slice_in_dim(mine, jnp.bitwise_and(z_lo + k, Z_LO - 1) * quarter, quarter, 1)
        for k in range(Z_LO)
    ]
    mine = [mine[0]] + [along_z_lo(mine[k], k) for k in range(1, Z_LO)]
    mine, hidden_grad = lax.optimization_barrier((mine, hidden_grad))
    hidden = [hidden_grad] + [along_z_lo(hidden_grad, k) for k in range(1, Z_LO)]
    mine = jnp.stack(mine)
    mine = lax.all_gather(mine, "mp", axis=1, axis_index_groups=X_GROUPS, tiled=True)
    patches = [
        lax.all_gather(mine[k : k + 2], "mp", axis=1, axis_index_groups=C_GROUPS, tiled=True)
        for k in range(0, Z_LO, 2)
    ]
    patches, hidden = lax.optimization_barrier((patches, hidden))
    patches = jnp.concatenate(patches, 0).reshape(Z_LO * rows, quarter)

    weight_part = lax.dot_general(
        patches,
        jnp.concatenate(hidden, 0),
        (((0,), (0,)), ((), ())),
        preferred_element_type=jnp.float32,
    ).astype(jnp.bfloat16)
    weight_part, hidden = lax.optimization_barrier((weight_part, hidden))
    received = lax.psum_scatter(
        weight_part, "fsdp", scatter_dimension=0, axis_index_groups=Y_GROUPS, tiled=True
    )
    grad_weight = (received.astype(jnp.float32) * norm_factor).astype(jnp.bfloat16)

    for_other, for_own = input_parts(own_place, hidden, weight)
    theirs = to_other_core(for_other)
    partial = (for_own.astype(jnp.float32) + theirs.astype(jnp.float32)).astype(jnp.bfloat16)
    partial = total(swap(partial, "mp", X_GROUPS))
    both = jnp.broadcast_to(partial[None], (Z_HI, Z_LO, piece, half))
    both = swap(both.reshape(Z_HI * Z_LO, piece, half), AXES, RING_GROUPS)
    mine = total(both.reshape(Z_HI, Z_LO, piece, half))
    mine = swap(jnp.broadcast_to(mine[None], (X, Z_LO, piece, half)), "mp", X_GROUPS)
    grad_input = joined(core.reshape(1), mine, to_other_core(mine))
    return (grad_weight, grad_input)


def solution(mesh):
    placed = (P("fsdp", None), P("fsdp", "mp"), P("fsdp", "mp"), P("fsdp", "mp"))
    return jax.shard_map(
        shards,
        mesh=mesh,
        in_specs=placed,
        out_specs=(P("fsdp", "mp"), P("fsdp", None)),
        check_vma=False,
    )
```

```python
import math

import jax
import jax.numpy as jnp
from jax import lax
from jax.experimental import pallas as pl
from jax.experimental.pallas import tpu as pltpu
from jax.sharding import PartitionSpec as P

Z_LO, Y = 4, 8
X, Z_HI, CORE = 4, 2, 2
AXES = ("fsdp", "mp")


def fsdp_index(z, y):
    return z * Y + y


def mp_index(x, h, c):
    return (x * Z_HI + h) * CORE + c


Z_GROUPS = [[fsdp_index(z, y) for z in range(Z_LO)] for y in range(Y)]
Y_GROUPS = [[fsdp_index(z, y) for y in range(Y)] for z in range(Z_LO)]
C_GROUPS = [[mp_index(x, h, c) for c in range(CORE)] for x in range(X) for h in range(Z_HI)]
X_GROUPS = [[mp_index(x, h, c) for x in range(X)] for h in range(Z_HI) for c in range(CORE)]
RING_GROUPS = [
    [fsdp_index(z, y) * (X * Z_HI * CORE) + mp_index(x, h, c) for h in range(Z_HI) for z in range(Z_LO)]
    for y in range(Y)
    for x in range(X)
    for c in range(CORE)
]


def moved(value, target):
    pairs = []
    for z in range(Z_LO):
        for y in range(Y):
            for x in range(X):
                for h in range(Z_HI):
                    for c in range(CORE):
                        z2, y2, x2, h2, c2 = target(z, y, x, h, c)
                        source = fsdp_index(z, y) * X * Z_HI * CORE + mp_index(x, h, c)
                        goal = fsdp_index(z2, y2) * X * Z_HI * CORE + mp_index(x2, h2, c2)
                        pairs.append((source, goal))
    return lax.ppermute(value, AXES, pairs)


def along_z_lo(value, step):
    return moved(value, lambda z, y, x, h, c: ((z + step) % Z_LO, y, x, h, c))


def to_other_core(value):
    return moved(value, lambda z, y, x, h, c: (z, y, x, h, 1 - c))


def gelu_slope(hidden):
    coeff = math.sqrt(2.0 / math.pi)
    inner = coeff * (hidden + 0.044715 * hidden * hidden * hidden)
    tangent = jnp.tanh(inner)
    return 0.5 * (1.0 + tangent) + 0.5 * hidden * (1.0 - tangent * tangent) * coeff * (
        1.0 + 3.0 * 0.044715 * hidden * hidden
    )


def swap(blocks, axis, groups):
    return lax.all_to_all(blocks, axis, 0, 0, axis_index_groups=groups, tiled=True)


def by_distance_kernel(place, blocks, out):
    for k in range(Z_LO):
        out[k] = blocks[jnp.bitwise_and(place[0] + (Z_LO - k), Z_LO - 1)]


def by_distance(place, blocks):
    return pl.pallas_call(
        by_distance_kernel,
        in_specs=[pl.BlockSpec(memory_space=pltpu.SMEM), pl.BlockSpec(memory_space=pltpu.VMEM)],
        out_specs=pl.BlockSpec(memory_space=pltpu.VMEM),
        out_shape=jax.ShapeDtypeStruct(blocks.shape, blocks.dtype),
        cost_estimate=pl.CostEstimate(flops=0, bytes_accessed=4 * blocks.size, transcendentals=0),
    )(place, blocks)


def input_parts_kernel(place, *refs):
    blocks, weight, outs = refs[:Z_LO], refs[Z_LO], refs[Z_LO + 1 :]
    rows = blocks[0].shape[0]
    piece = rows // X
    half = weight.shape[0] // CORE
    lhs = jnp.concatenate([block[...] for block in blocks], axis=0)
    for out, which in zip(outs, (1 - place[1], place[1])):
        result = lax.dot_general(
            lhs,
            weight[pl.ds(pl.multiple_of(which * half, half), half), :],
            (((1,), (1,)), ((), ())),
            preferred_element_type=jnp.float32,
        )
        for k in range(Z_LO):
            owner = jnp.bitwise_and(place[0] + (Z_LO - k), Z_LO - 1)
            for x in range(X):
                start = k * rows + x * piece
                out[x, owner] = result[start : start + piece].astype(out.dtype)


def input_parts(place, blocks, weight):
    rows, units = blocks[0].shape
    half = weight.shape[0] // CORE
    out = jax.ShapeDtypeStruct((X, Z_LO, rows // X, half), jnp.bfloat16)
    return pl.pallas_call(
        input_parts_kernel,
        in_specs=[pl.BlockSpec(memory_space=pltpu.SMEM)]
        + [pl.BlockSpec(memory_space=pltpu.VMEM)] * (Z_LO + 1),
        out_specs=[pl.BlockSpec(memory_space=pltpu.VMEM)] * 2,
        out_shape=[out, out],
        compiler_params=pltpu.CompilerParams(vmem_limit_bytes=32 * 1024 * 1024),
        cost_estimate=pl.CostEstimate(
            flops=4 * Z_LO * rows * units * half,
            bytes_accessed=2 * (Z_LO * rows * units + 2 * half * units + 2 * Z_LO * rows * half),
            transcendentals=0,
        ),
    )(place, *blocks, weight)


def joined_kernel(core, mine, theirs, out):
    blocks, quarters, piece, half = mine.shape
    for own in range(CORE):

        @pl.when(core[0] == own)
        def _():
            for x in range(blocks):
                for z in range(quarters):
                    for c in range(CORE):
                        start = (z * CORE + c) * half
                        out[x * piece : (x + 1) * piece, start : start + half] = (
                            mine if c == own else theirs
                        )[x, z]


def joined(core, mine, theirs):
    x, z, piece, half = mine.shape
    return pl.pallas_call(
        joined_kernel,
        in_specs=[
            pl.BlockSpec(memory_space=pltpu.SMEM),
            pl.BlockSpec(memory_space=pltpu.VMEM),
            pl.BlockSpec(memory_space=pltpu.VMEM),
        ],
        out_specs=pl.BlockSpec(memory_space=pltpu.VMEM),
        out_shape=jax.ShapeDtypeStruct((x * piece, z * CORE * half), mine.dtype),
        compiler_params=pltpu.CompilerParams(vmem_limit_bytes=32 * 1024 * 1024),
        cost_estimate=pl.CostEstimate(
            flops=0, bytes_accessed=4 * CORE * mine.size, transcendentals=0
        ),
    )(core, mine, theirs)


def total(blocks):
    return jnp.sum(blocks.astype(jnp.float32), axis=0).astype(jnp.bfloat16)


def shards(tokens, pre_act, grad_act, w_up):
    rows, width = tokens.shape
    units = pre_act.shape[1]
    quarter = width // Z_LO
    half = quarter // CORE
    piece = rows // X
    norm_factor = float(rows * Z_LO * Y) ** (-0.5)
    z_lo = lax.shift_right_logical(lax.axis_index("fsdp"), 3)
    x = lax.shift_right_logical(lax.axis_index("mp"), 2)
    core = jnp.bitwise_and(lax.axis_index("mp"), 1)
    own_place = jnp.stack([z_lo, core])

    weight = lax.all_gather(w_up, "fsdp", axis=0, axis_index_groups=Y_GROUPS, tiled=True)
    hidden_grad = (grad_act.astype(jnp.float32) * gelu_slope(pre_act.astype(jnp.float32))).astype(
        jnp.bfloat16
    )
    part = rows // (CORE * X)
    mine = lax.dynamic_slice_in_dim(tokens, (core * X + x) * part, part, 0)
    mine = swap(mine.reshape(part, Z_LO, quarter).transpose(1, 0, 2), "fsdp", Z_GROUPS)
    mine, hidden_grad = lax.optimization_barrier((mine, hidden_grad))
    hidden = [hidden_grad] + [along_z_lo(hidden_grad, k) for k in range(1, Z_LO)]
    mine = by_distance(z_lo.reshape(1), mine)
    mine = lax.all_gather(mine, "mp", axis=1, axis_index_groups=X_GROUPS, tiled=True)
    patches = [
        lax.all_gather(mine[k : k + 2], "mp", axis=1, axis_index_groups=C_GROUPS, tiled=True)
        for k in range(0, Z_LO, 2)
    ]
    patches, hidden = lax.optimization_barrier((patches, hidden))
    patches = jnp.concatenate(patches, 0).reshape(Z_LO * rows, quarter)

    weight_part = lax.dot_general(
        patches,
        jnp.concatenate(hidden, 0),
        (((0,), (0,)), ((), ())),
        preferred_element_type=jnp.float32,
    ).astype(jnp.bfloat16)
    weight_part, hidden = lax.optimization_barrier((weight_part, hidden))
    received = lax.psum_scatter(
        weight_part, "fsdp", scatter_dimension=0, axis_index_groups=Y_GROUPS, tiled=True
    )
    grad_weight = (received.astype(jnp.float32) * norm_factor).astype(jnp.bfloat16)

    for_other, for_own = input_parts(own_place, hidden, weight)
    theirs = to_other_core(for_other)
    partial = (for_own.astype(jnp.float32) + theirs.astype(jnp.float32)).astype(jnp.bfloat16)
    partial = total(swap(partial, "mp", X_GROUPS))
    both = jnp.broadcast_to(partial[None], (Z_HI, Z_LO, piece, half))
    both = swap(both.reshape(Z_HI * Z_LO, piece, half), AXES, RING_GROUPS)
    mine = total(both.reshape(Z_HI, Z_LO, piece, half))
    mine = swap(jnp.broadcast_to(mine[None], (X, Z_LO, piece, half)), "mp", X_GROUPS)
    grad_input = joined(core.reshape(1), mine, to_other_core(mine))
    return (grad_weight, grad_input)


def solution(mesh):
    placed = (P("fsdp", None), P("fsdp", "mp"), P("fsdp", "mp"), P("fsdp", "mp"))
    return jax.shard_map(
        shards,
        mesh=mesh,
        in_specs=placed,
        out_specs=(P("fsdp", "mp"), P("fsdp", None)),
        check_vma=False,
    )
```

```python
import math

import jax
import jax.numpy as jnp
from jax import lax
from jax.experimental import pallas as pl
from jax.experimental.pallas import tpu as pltpu
from jax.sharding import PartitionSpec as P

Z_LO, Y = 4, 8
X, Z_HI, CORE = 4, 2, 2
AXES = ("fsdp", "mp")


def fsdp_index(z, y):
    return z * Y + y


def mp_index(x, h, c):
    return (x * Z_HI + h) * CORE + c


Z_GROUPS = [[fsdp_index(z, y) for z in range(Z_LO)] for y in range(Y)]
Y_GROUPS = [[fsdp_index(z, y) for y in range(Y)] for z in range(Z_LO)]
C_GROUPS = [[mp_index(x, h, c) for c in range(CORE)] for x in range(X) for h in range(Z_HI)]
X_GROUPS = [[mp_index(x, h, c) for x in range(X)] for h in range(Z_HI) for c in range(CORE)]
RING_GROUPS = [
    [fsdp_index(z, y) * (X * Z_HI * CORE) + mp_index(x, h, c) for h in range(Z_HI) for z in range(Z_LO)]
    for y in range(Y)
    for x in range(X)
    for c in range(CORE)
]


def moved(value, target):
    pairs = []
    for z in range(Z_LO):
        for y in range(Y):
            for x in range(X):
                for h in range(Z_HI):
                    for c in range(CORE):
                        z2, y2, x2, h2, c2 = target(z, y, x, h, c)
                        source = fsdp_index(z, y) * X * Z_HI * CORE + mp_index(x, h, c)
                        goal = fsdp_index(z2, y2) * X * Z_HI * CORE + mp_index(x2, h2, c2)
                        pairs.append((source, goal))
    return lax.ppermute(value, AXES, pairs)


def along_z_lo(value, step):
    return moved(value, lambda z, y, x, h, c: ((z + step) % Z_LO, y, x, h, c))


def to_other_core(value):
    return moved(value, lambda z, y, x, h, c: (z, y, x, h, 1 - c))


def gelu_slope(hidden):
    coeff = math.sqrt(2.0 / math.pi)
    inner = coeff * (hidden + 0.044715 * hidden * hidden * hidden)
    tangent = jnp.tanh(inner)
    return 0.5 * (1.0 + tangent) + 0.5 * hidden * (1.0 - tangent * tangent) * coeff * (
        1.0 + 3.0 * 0.044715 * hidden * hidden
    )


def swap(blocks, axis, groups):
    return lax.all_to_all(blocks, axis, 0, 0, axis_index_groups=groups, tiled=True)


def by_distance_kernel(place, blocks, out):
    for k in range(Z_LO):
        out[k] = blocks[jnp.bitwise_and(place[0] + (Z_LO - k), Z_LO - 1)]


def by_distance(place, blocks):
    return pl.pallas_call(
        by_distance_kernel,
        in_specs=[pl.BlockSpec(memory_space=pltpu.SMEM), pl.BlockSpec(memory_space=pltpu.VMEM)],
        out_specs=pl.BlockSpec(memory_space=pltpu.VMEM),
        out_shape=jax.ShapeDtypeStruct(blocks.shape, blocks.dtype),
        cost_estimate=pl.CostEstimate(flops=0, bytes_accessed=4 * blocks.size, transcendentals=0),
    )(place, blocks)


def input_part_kernel(place, *refs):
    blocks, weight, out, chosen, arrived = refs[:Z_LO], refs[Z_LO], refs[-3], refs[-2], refs[-1]
    rows = blocks[0].shape[0]
    piece = rows // X
    half = chosen.shape[0]
    copy = pltpu.make_async_copy(
        weight.at[pl.ds(pl.multiple_of(place[1] * half, half), half)], chosen, arrived
    )
    copy.start()
    lhs = jnp.concatenate([block[...] for block in blocks], axis=0)
    copy.wait()
    result = lax.dot_general(
        lhs, chosen[...], (((1,), (1,)), ((), ())), preferred_element_type=jnp.float32
    )
    for k in range(Z_LO):
        owner = jnp.bitwise_and(place[0] + (Z_LO - k), Z_LO - 1)
        for x in range(X):
            start = k * rows + x * piece
            out[x, owner] = result[start : start + piece].astype(out.dtype)


def input_part(place, blocks, weight):
    rows, units = blocks[0].shape
    half = weight.shape[0] // CORE
    return pl.pallas_call(
        input_part_kernel,
        in_specs=[pl.BlockSpec(memory_space=pltpu.SMEM)]
        + [pl.BlockSpec(memory_space=pltpu.VMEM)] * Z_LO
        + [pl.BlockSpec(memory_space=pltpu.HBM)],
        out_specs=pl.BlockSpec(memory_space=pltpu.VMEM),
        out_shape=jax.ShapeDtypeStruct((X, Z_LO, rows // X, half), jnp.bfloat16),
        scratch_shapes=[pltpu.VMEM((half, units), jnp.bfloat16), pltpu.SemaphoreType.DMA],
        compiler_params=pltpu.CompilerParams(vmem_limit_bytes=32 * 1024 * 1024),
        cost_estimate=pl.CostEstimate(
            flops=2 * Z_LO * rows * units * half,
            bytes_accessed=2 * (Z_LO * rows * units + half * units + Z_LO * rows * half),
            transcendentals=0,
        ),
    )(place, *blocks, pltpu.with_memory_space_constraint(weight, pltpu.HBM))


def joined_kernel(core, mine, theirs, out):
    blocks, quarters, piece, half = mine.shape
    for own in range(CORE):

        @pl.when(core[0] == own)
        def _():
            for x in range(blocks):
                for z in range(quarters):
                    for c in range(CORE):
                        start = (z * CORE + c) * half
                        out[x * piece : (x + 1) * piece, start : start + half] = (
                            mine if c == own else theirs
                        )[x, z]


def joined(core, mine, theirs):
    x, z, piece, half = mine.shape
    return pl.pallas_call(
        joined_kernel,
        in_specs=[
            pl.BlockSpec(memory_space=pltpu.SMEM),
            pl.BlockSpec(memory_space=pltpu.VMEM),
            pl.BlockSpec(memory_space=pltpu.VMEM),
        ],
        out_specs=pl.BlockSpec(memory_space=pltpu.VMEM),
        out_shape=jax.ShapeDtypeStruct((x * piece, z * CORE * half), mine.dtype),
        compiler_params=pltpu.CompilerParams(vmem_limit_bytes=32 * 1024 * 1024),
        cost_estimate=pl.CostEstimate(
            flops=0, bytes_accessed=4 * CORE * mine.size, transcendentals=0
        ),
    )(core, mine, theirs)


def total(blocks):
    return jnp.sum(blocks.astype(jnp.float32), axis=0).astype(jnp.bfloat16)


def shards(tokens, pre_act, grad_act, w_up):
    rows, width = tokens.shape
    units = pre_act.shape[1]
    quarter = width // Z_LO
    half = quarter // CORE
    piece = rows // X
    norm_factor = float(rows * Z_LO * Y) ** (-0.5)
    z_lo = lax.shift_right_logical(lax.axis_index("fsdp"), 3)
    x = lax.shift_right_logical(lax.axis_index("mp"), 2)
    core = jnp.bitwise_and(lax.axis_index("mp"), 1)
    theirs_place = jnp.stack([z_lo, 1 - core])
    own_place = jnp.stack([z_lo, core])

    weight = lax.all_gather(w_up, "fsdp", axis=0, axis_index_groups=Y_GROUPS, tiled=True)
    hidden_grad = (grad_act.astype(jnp.float32) * gelu_slope(pre_act.astype(jnp.float32))).astype(
        jnp.bfloat16
    )
    part = rows // (CORE * X)
    mine = lax.dynamic_slice_in_dim(tokens, (core * X + x) * part, part, 0)
    mine = swap(mine.reshape(part, Z_LO, quarter).transpose(1, 0, 2), "fsdp", Z_GROUPS)
    mine, hidden_grad = lax.optimization_barrier((mine, hidden_grad))
    hidden = [hidden_grad] + [along_z_lo(hidden_grad, k) for k in range(1, Z_LO)]
    mine = by_distance(z_lo.reshape(1), mine)
    mine = lax.all_gather(mine, "mp", axis=1, axis_index_groups=X_GROUPS, tiled=True)
    patches = [
        lax.all_gather(mine[k : k + 2], "mp", axis=1, axis_index_groups=C_GROUPS, tiled=True)
        for k in range(0, Z_LO, 2)
    ]
    patches, hidden = lax.optimization_barrier((patches, hidden))
    patches = jnp.concatenate(patches, 0).reshape(Z_LO * rows, quarter)

    weight_part = lax.dot_general(
        patches,
        jnp.concatenate(hidden, 0),
        (((0,), (0,)), ((), ())),
        preferred_element_type=jnp.float32,
    ).astype(jnp.bfloat16)
    weight_part, hidden = lax.optimization_barrier((weight_part, hidden))
    received = lax.psum_scatter(
        weight_part, "fsdp", scatter_dimension=0, axis_index_groups=Y_GROUPS, tiled=True
    )
    grad_weight = (received.astype(jnp.float32) * norm_factor).astype(jnp.bfloat16)

    theirs = to_other_core(input_part(theirs_place, hidden, weight))
    partial = input_part(own_place, hidden, weight)
    partial = (partial.astype(jnp.float32) + theirs.astype(jnp.float32)).astype(jnp.bfloat16)
    partial = total(swap(partial, "mp", X_GROUPS))
    both = jnp.broadcast_to(partial[None], (Z_HI, Z_LO, piece, half))
    both = swap(both.reshape(Z_HI * Z_LO, piece, half), AXES, RING_GROUPS)
    mine = total(both.reshape(Z_HI, Z_LO, piece, half))
    mine = swap(jnp.broadcast_to(mine[None], (X, Z_LO, piece, half)), "mp", X_GROUPS)
    grad_input = joined(core.reshape(1), mine, to_other_core(mine))
    return (grad_weight, grad_input)


def solution(mesh):
    placed = (P("fsdp", None), P("fsdp", "mp"), P("fsdp", "mp"), P("fsdp", "mp"))
    return jax.shard_map(
        shards,
        mesh=mesh,
        in_specs=placed,
        out_specs=(P("fsdp", "mp"), P("fsdp", None)),
        check_vma=False,
    )
```

```python
import math

import jax
import jax.numpy as jnp
from jax import lax
from jax.experimental import pallas as pl
from jax.experimental.pallas import tpu as pltpu
from jax.sharding import PartitionSpec as P

Z_LO, Y = 4, 8
X, Z_HI, CORE = 4, 2, 2
AXES = ("fsdp", "mp")


def fsdp_index(z, y):
    return z * Y + y


def mp_index(x, h, c):
    return (x * Z_HI + h) * CORE + c


Z_GROUPS = [[fsdp_index(z, y) for z in range(Z_LO)] for y in range(Y)]
Y_GROUPS = [[fsdp_index(z, y) for y in range(Y)] for z in range(Z_LO)]
C_GROUPS = [[mp_index(x, h, c) for c in range(CORE)] for x in range(X) for h in range(Z_HI)]
X_GROUPS = [[mp_index(x, h, c) for x in range(X)] for h in range(Z_HI) for c in range(CORE)]
RING_GROUPS = [
    [fsdp_index(z, y) * (X * Z_HI * CORE) + mp_index(x, h, c) for h in range(Z_HI) for z in range(Z_LO)]
    for y in range(Y)
    for x in range(X)
    for c in range(CORE)
]


def moved(value, target):
    pairs = []
    for z in range(Z_LO):
        for y in range(Y):
            for x in range(X):
                for h in range(Z_HI):
                    for c in range(CORE):
                        z2, y2, x2, h2, c2 = target(z, y, x, h, c)
                        source = fsdp_index(z, y) * X * Z_HI * CORE + mp_index(x, h, c)
                        goal = fsdp_index(z2, y2) * X * Z_HI * CORE + mp_index(x2, h2, c2)
                        pairs.append((source, goal))
    return lax.ppermute(value, AXES, pairs)


def along_z_lo(value, step):
    return moved(value, lambda z, y, x, h, c: ((z + step) % Z_LO, y, x, h, c))


def to_other_core(value):
    return moved(value, lambda z, y, x, h, c: (z, y, x, h, 1 - c))


def gelu_slope(hidden):
    coeff = math.sqrt(2.0 / math.pi)
    inner = coeff * (hidden + 0.044715 * hidden * hidden * hidden)
    tangent = jnp.tanh(inner)
    return 0.5 * (1.0 + tangent) + 0.5 * hidden * (1.0 - tangent * tangent) * coeff * (
        1.0 + 3.0 * 0.044715 * hidden * hidden
    )


def swap(blocks, axis, groups):
    return lax.all_to_all(blocks, axis, 0, 0, axis_index_groups=groups, tiled=True)


def by_distance_kernel(place, blocks, out):
    for k in range(Z_LO):
        out[k] = blocks[jnp.bitwise_and(place[0] + (Z_LO - k), Z_LO - 1)]


def by_distance(place, blocks):
    return pl.pallas_call(
        by_distance_kernel,
        in_specs=[pl.BlockSpec(memory_space=pltpu.SMEM), pl.BlockSpec(memory_space=pltpu.VMEM)],
        out_specs=pl.BlockSpec(memory_space=pltpu.VMEM),
        out_shape=jax.ShapeDtypeStruct(blocks.shape, blocks.dtype),
        cost_estimate=pl.CostEstimate(flops=0, bytes_accessed=4 * blocks.size, transcendentals=0),
    )(place, blocks)


def input_parts_kernel(place, *refs):
    blocks, weight, outs = refs[:Z_LO], refs[Z_LO], refs[Z_LO + 1 : Z_LO + 1 + CORE]
    chosen, arrived = refs[-2], refs[-1]
    rows = blocks[0].shape[0]
    piece = rows // X
    half = chosen.shape[1]
    copies = [
        pltpu.make_async_copy(
            weight.at[pl.ds(pl.multiple_of(which * half, half), half)], chosen.at[i], arrived.at[i]
        )
        for i, which in enumerate((1 - place[1], place[1]))
    ]
    copies[0].start()
    lhs = jnp.concatenate([block[...] for block in blocks], axis=0)
    for i, out in enumerate(outs):
        copies[i].wait()
        if i + 1 < len(copies):
            copies[i + 1].start()
        result = lax.dot_general(
            lhs, chosen[i], (((1,), (1,)), ((), ())), preferred_element_type=jnp.float32
        )
        for k in range(Z_LO):
            owner = jnp.bitwise_and(place[0] + (Z_LO - k), Z_LO - 1)
            for x in range(X):
                start = k * rows + x * piece
                out[x, owner] = result[start : start + piece].astype(out.dtype)


def input_parts(place, blocks, weight):
    rows, units = blocks[0].shape
    half = weight.shape[0] // CORE
    out = jax.ShapeDtypeStruct((X, Z_LO, rows // X, half), jnp.bfloat16)
    return pl.pallas_call(
        input_parts_kernel,
        in_specs=[pl.BlockSpec(memory_space=pltpu.SMEM)]
        + [pl.BlockSpec(memory_space=pltpu.VMEM)] * Z_LO
        + [pl.BlockSpec(memory_space=pltpu.HBM)],
        out_specs=[pl.BlockSpec(memory_space=pltpu.VMEM)] * CORE,
        out_shape=[out] * CORE,
        scratch_shapes=[
            pltpu.VMEM((CORE, half, units), jnp.bfloat16),
            pltpu.SemaphoreType.DMA((CORE,)),
        ],
        compiler_params=pltpu.CompilerParams(vmem_limit_bytes=32 * 1024 * 1024),
        cost_estimate=pl.CostEstimate(
            flops=4 * Z_LO * rows * units * half,
            bytes_accessed=2 * (Z_LO * rows * units + 2 * half * units + 2 * Z_LO * rows * half),
            transcendentals=0,
        ),
    )(place, *blocks, pltpu.with_memory_space_constraint(weight, pltpu.HBM))


def joined_kernel(core, mine, theirs, out):
    blocks, quarters, piece, half = mine.shape
    for own in range(CORE):

        @pl.when(core[0] == own)
        def _():
            for x in range(blocks):
                for z in range(quarters):
                    for c in range(CORE):
                        start = (z * CORE + c) * half
                        out[x * piece : (x + 1) * piece, start : start + half] = (
                            mine if c == own else theirs
                        )[x, z]


def joined(core, mine, theirs):
    x, z, piece, half = mine.shape
    return pl.pallas_call(
        joined_kernel,
        in_specs=[
            pl.BlockSpec(memory_space=pltpu.SMEM),
            pl.BlockSpec(memory_space=pltpu.VMEM),
            pl.BlockSpec(memory_space=pltpu.VMEM),
        ],
        out_specs=pl.BlockSpec(memory_space=pltpu.VMEM),
        out_shape=jax.ShapeDtypeStruct((x * piece, z * CORE * half), mine.dtype),
        compiler_params=pltpu.CompilerParams(vmem_limit_bytes=32 * 1024 * 1024),
        cost_estimate=pl.CostEstimate(
            flops=0, bytes_accessed=4 * CORE * mine.size, transcendentals=0
        ),
    )(core, mine, theirs)


def total(blocks):
    return jnp.sum(blocks.astype(jnp.float32), axis=0).astype(jnp.bfloat16)


def shards(tokens, pre_act, grad_act, w_up):
    rows, width = tokens.shape
    units = pre_act.shape[1]
    quarter = width // Z_LO
    half = quarter // CORE
    piece = rows // X
    norm_factor = float(rows * Z_LO * Y) ** (-0.5)
    z_lo = lax.shift_right_logical(lax.axis_index("fsdp"), 3)
    x = lax.shift_right_logical(lax.axis_index("mp"), 2)
    core = jnp.bitwise_and(lax.axis_index("mp"), 1)
    own_place = jnp.stack([z_lo, core])

    weight = lax.all_gather(w_up, "fsdp", axis=0, axis_index_groups=Y_GROUPS, tiled=True)
    hidden_grad = (grad_act.astype(jnp.float32) * gelu_slope(pre_act.astype(jnp.float32))).astype(
        jnp.bfloat16
    )
    part = rows // (CORE * X)
    mine = lax.dynamic_slice_in_dim(tokens, (core * X + x) * part, part, 0)
    mine = swap(mine.reshape(part, Z_LO, quarter).transpose(1, 0, 2), "fsdp", Z_GROUPS)
    mine, hidden_grad = lax.optimization_barrier((mine, hidden_grad))
    hidden = [hidden_grad] + [along_z_lo(hidden_grad, k) for k in range(1, Z_LO)]
    mine = by_distance(z_lo.reshape(1), mine)
    mine = lax.all_gather(mine, "mp", axis=1, axis_index_groups=X_GROUPS, tiled=True)
    patches = [
        lax.all_gather(mine[k : k + 2], "mp", axis=1, axis_index_groups=C_GROUPS, tiled=True)
        for k in range(0, Z_LO, 2)
    ]
    patches, hidden = lax.optimization_barrier((patches, hidden))
    patches = jnp.concatenate(patches, 0).reshape(Z_LO * rows, quarter)

    weight_part = lax.dot_general(
        patches,
        jnp.concatenate(hidden, 0),
        (((0,), (0,)), ((), ())),
        preferred_element_type=jnp.float32,
    ).astype(jnp.bfloat16)
    weight_part, hidden = lax.optimization_barrier((weight_part, hidden))
    received = lax.psum_scatter(
        weight_part, "fsdp", scatter_dimension=0, axis_index_groups=Y_GROUPS, tiled=True
    )
    grad_weight = (received.astype(jnp.float32) * norm_factor).astype(jnp.bfloat16)

    for_other, for_own = input_parts(own_place, hidden, weight)
    theirs = to_other_core(for_other)
    partial = (for_own.astype(jnp.float32) + theirs.astype(jnp.float32)).astype(jnp.bfloat16)
    partial = total(swap(partial, "mp", X_GROUPS))
    both = jnp.broadcast_to(partial[None], (Z_HI, Z_LO, piece, half))
    both = swap(both.reshape(Z_HI * Z_LO, piece, half), AXES, RING_GROUPS)
    mine = total(both.reshape(Z_HI, Z_LO, piece, half))
    mine = swap(jnp.broadcast_to(mine[None], (X, Z_LO, piece, half)), "mp", X_GROUPS)
    grad_input = joined(core.reshape(1), mine, to_other_core(mine))
    return (grad_weight, grad_input)


def solution(mesh):
    placed = (P("fsdp", None), P("fsdp", "mp"), P("fsdp", "mp"), P("fsdp", "mp"))
    return jax.shard_map(
        shards,
        mesh=mesh,
        in_specs=placed,
        out_specs=(P("fsdp", "mp"), P("fsdp", None)),
        check_vma=False,
    )
```
